512 devices in a mesh: blk: 128 (over z_lo, x, y), red: 4 (over z_hi, core).
Axes of the slice: x: 4, y: 4, z: 16 (z_hi: 2, z_lo: 8; z = z_hi * 8 + z_lo), core: 2. Of those that a mesh axis runs over, the one named last changes fastest.
Arguments:
- amplitudes: bfloat16 [8192, 16384], P('blk', 'red'), may hold values from -6 to 6
- integrals: bfloat16 [65536, 16384], P('blk', 'red'), may hold values from -0.046875 to 0.046875
- occ_live: int32 [8], replicated, may hold values from 256 to 1024, as said below
Outputs:
- residual: bfloat16 [1024, 65536], P('red', 'blk')
The draws below stay inside these ranges and needn't reach their ends.
Inputs may be any that keep to these rules, and one draw needn't show every extreme that they name: Rows ij at or past occ_live[s] of sector s are padding; some sector is always full, with 1024 live pairs.
All inputs are finite; a program needn't handle non-finite values.
Results may differ from the reference program's by a relative error of at most 0.001.
Values may be sent and summed in bfloat16 or wider, within the bound.
No kernel may reach another device: no remote copies, remote signals or barrier semaphores. Data moves between devices by JAX's collectives and lax.ppermute only.
A program may use at most 128 MiB of HBM per device.

```python
import jax
import jax.numpy as jnp
from jax import lax

CD = 16384
SECT = 8
AB_SEC = 8192
IJ_SEC = 1024


def draw_occ_live(key, part):
    key = jax.random.fold_in(key, 7)
    first, second = jax.random.split(key)
    counts = jax.random.randint(first, (SECT,), IJ_SEC // 4, IJ_SEC + 1)
    fullest = jax.random.randint(second, (), 0, SECT)
    return jnp.where(jnp.arange(SECT) == fullest, IJ_SEC, counts).astype(jnp.int32)


def levels(rng, shape, shards, smallest, largest):
    factor_of, own = 1.0, jax.random.fold_in(rng, 6)
    for dim, blocks in shards:
        steps = jnp.exp(jax.random.uniform(jax.random.fold_in(own, dim), (blocks,), jnp.float32, smallest / len(shards), largest / len(shards)))
        factor_of = factor_of * jnp.repeat(steps, shape[dim] // blocks).reshape([-1 if axis == dim else 1 for axis in range(len(shape))])
    return factor_of


def scatter_about(stream_key, extent, scale, reach, cuts=(), kind=jnp.bfloat16):
    gain = levels(stream_key, extent, cuts, -0.22, 0.18) if cuts else 1.0
    drawn = jax.random.normal(stream_key, extent, jnp.float32) * scale * gain
    return jnp.minimum(jnp.maximum(drawn, -reach), reach).astype(kind)


def setup_inputs(seed: int = 0) -> dict:
    arg_keys = jax.random.split(jax.random.key(seed), 4)
    amplitudes = scatter_about(arg_keys[0], (SECT * IJ_SEC, CD), 1.0, 6.0, ((0, 128), (1, 4)))
    integrals = scatter_about(arg_keys[1], (SECT * AB_SEC, CD), CD ** -0.5, 0.046875, ((0, 128), (1, 4)))
    occ_live = draw_occ_live(jax.random.fold_in(arg_keys[3], 71), 0)
    return {"amplitudes": amplitudes, "integrals": integrals, "occ_live": occ_live}


def reference(amplitudes, integrals, occ_live):
    row_index = jnp.arange(IJ_SEC, dtype=jnp.int32)

    def one_sector(sector):
        start_ij = (sector * IJ_SEC).astype(jnp.int32)
        start_ab = (sector * AB_SEC).astype(jnp.int32)
        pairs = lax.dynamic_slice_in_dim(amplitudes, start_ij, IJ_SEC, 0)
        tiles = lax.dynamic_slice_in_dim(integrals, start_ab, AB_SEC, 0)
        product = lax.dot_general(pairs, tiles, (((1,), (1,)), ((), ())), preferred_element_type=jnp.float32)
        live = lax.dynamic_index_in_dim(occ_live, sector, 0, keepdims=False)
        kept = jnp.where((row_index < live)[:, None], product, jnp.zeros((), product.dtype))
        return kept.astype(jnp.bfloat16)

    blocks = lax.map(one_sector, jnp.arange(SECT, dtype=jnp.int32))
    return jnp.transpose(blocks, (1, 0, 2)).reshape(IJ_SEC, SECT * AB_SEC)
```

```python
import jax
import jax.numpy as jnp
from jax import lax
from jax.sharding import PartitionSpec as P

LANES = 128


def power_steps():
    return [(float(2**j), 2.0 ** (2**j), 2.0 ** -(2**j)) for j in (6, 5, 4, 3, 2, 1)]


def scaled_rows(block):
    wide = block.astype(jnp.float32)
    largest = jnp.max(jnp.abs(wide), axis=1, keepdims=True)
    scale = jnp.ones_like(largest)
    exponent = jnp.zeros_like(largest)
    for step, up, _ in power_steps():
        fits = largest * scale * up <= 32768.0
        scale = jnp.where(fits, scale * up, scale)
        exponent = jnp.where(fits, exponent + step, exponent)
    rows = (wide * scale).astype(jnp.float16)
    tail = jnp.broadcast_to(exponent, (block.shape[0], LANES)).astype(jnp.float16)
    return jnp.concatenate([rows, tail], 1)


def unscale(exponent):
    left = exponent.astype(jnp.float32)
    factor = jnp.ones_like(left)
    for step, _, down in power_steps():
        taken = left >= step
        factor = jnp.where(taken, factor * down, factor)
        left = jnp.where(taken, left - step, left)
    return factor


def on_device(amplitudes, integrals, occ_live):
    ij_dev, cd_dev = amplitudes.shape
    n_blk, n_red = lax.axis_size("blk"), lax.axis_size("red")
    group = 16
    planes = [[s * group + m for m in range(group)] for s in range(n_blk // group)]
    ij_sec = ij_dev * group
    rows_red = ij_sec // n_red
    half = ij_sec // 2
    red = lax.axis_index("red")
    z_half, core = red // 2, red % 2
    sector = lax.axis_index("blk") // group
    live = jnp.sum(jnp.where(jnp.arange(occ_live.shape[0]) == sector, occ_live, 0))

    gathered = lax.all_gather(
        scaled_rows(amplitudes), "blk", axis_index_groups=planes, axis=0, tiled=True
    )

    def partial_rows(start):
        rows = lax.dynamic_slice_in_dim(gathered, start, half, 0)
        product = lax.dot_general(
            rows[:, :cd_dev].astype(jnp.bfloat16),
            integrals,
            (((1,), (1,)), ((), ())),
            preferred_element_type=jnp.float32,
        )
        product = product * unscale(rows[:, cd_dev : cd_dev + 1])
        return product.reshape(2, rows_red, product.shape[1])

    def core_sum(parts):
        mine = jnp.where(core == 0, parts[0], parts[1])
        other = jnp.where(core == 0, parts[1], parts[0])
        got = lax.ppermute(other, "red", [(r, r ^ 1) for r in range(n_red)])
        return mine + got

    away = core_sum(partial_rows((1 - z_half) * half))
    came = lax.ppermute(away, "red", [(r, r ^ 2) for r in range(n_red)])
    summed = core_sum(partial_rows(z_half * half)) + came
    my_rows = red * rows_red + jnp.arange(rows_red, dtype=jnp.int32)
    kept = jnp.where((my_rows < live)[:, None], summed, jnp.zeros((), jnp.float32))
    return kept.astype(jnp.bfloat16)


def solution(mesh):
    in_specs = (P("blk", "red"), P("blk", "red"), P())
    out_specs = P("red", "blk")
    return jax.shard_map(
        on_device, mesh=mesh, in_specs=in_specs, out_specs=out_specs, check_vma=False
    )
```

```python
import jax
import jax.numpy as jnp
from jax import lax
from jax.sharding import PartitionSpec as P

GROUP = 16
AXES = ("blk", "red")


def halves(block):
    middle = block.shape[0] // 2
    return block[:middle], block[middle:]


def join(*blocks):
    return jnp.concatenate(blocks, 0)


def hop(block, mask_first, mask_second):
    n_blk, n_red = lax.axis_size("blk"), lax.axis_size("red")
    route = []
    for b in range(n_blk):
        for r in range(n_red):
            route.append((b * n_red + r, (b ^ (mask_second if r % 2 else mask_first)) * n_red + r))
    return lax.ppermute(block, AXES, route)


def between_cores(block):
    return lax.ppermute(block, "red", [(r, r ^ 1) for r in range(lax.axis_size("red"))])


def between_planes(block, sends):
    n_blk, n_red = lax.axis_size("blk"), lax.axis_size("red")
    route = []
    for b in range(n_blk):
        for r in range(n_red):
            early = (b % GROUP) // 8 != r // 2
            if sends(r % 2, early):
                route.append((b * n_red + r, b * n_red + (r ^ 2)))
    return lax.ppermute(block, AXES, route)


def on_device(amplitudes, integrals, occ_live):
    ij_dev, cd_dev = amplitudes.shape
    blk, red = lax.axis_index("blk"), lax.axis_index("red")
    first = red % 2 == 0
    z_half = red // 2
    sector, member = blk // GROUP, blk % GROUP
    x, y = member // 4, member % 4
    same = x // 2 == z_half
    live = jnp.sum(jnp.where(jnp.arange(occ_live.shape[0]) == sector, occ_live, 0))

    with jax.named_scope("swap"):
        low, high = halves(amplitudes)
        got = between_cores(jnp.where(first, high, low))
        own = jnp.concatenate([jnp.where(first, low, high), got], 1)
        integrals_other = between_cores(integrals)

    with jax.named_scope("line"):
        line_b = hop(own, 12, 3)
        line_a = hop(own, 4, 1)
        line_c = hop(own, 8, 2)
        outer = join(own, line_b)
        inner = join(line_a, line_c)
    with jax.named_scope("plane"):
        a_outer, b_outer = hop(outer, 1, 4), hop(outer, 3, 12)
        a_inner, b_inner = hop(inner, 1, 4), hop(inner, 3, 12)
        c_outer, c_inner = hop(b_outer, 1, 4), hop(a_inner, 3, 12)

    def product(one, two):
        rows = join(one, two)
        dims = (((1,), (1,)), ((), ()))
        total = lax.dot_general(
            rows[:, :cd_dev], integrals, dims, preferred_element_type=jnp.float32
        ) + lax.dot_general(
            rows[:, cd_dev:], integrals_other, dims, preferred_element_type=jnp.float32
        )
        return halves(total)

    pairs = [(outer, inner), (a_outer, b_outer), (a_inner, b_inner), (c_outer, c_inner)]
    with jax.named_scope("products"):
        made = [product(*pair) for pair in pairs]
    (p_outer, p_inner), (pa_outer, pb_outer), (pa_inner, pb_inner), (pc_outer, pc_inner) = made

    mine, away = [], []
    for one, two in made:
        parts = [halves(one), halves(two)]
        mine.append(join(*[jnp.where(same, near, far) for near, far in parts]))
        away.append(join(*[jnp.where(same, far, near) for near, far in parts]))
    near = [p_outer, p_inner, pa_outer, pa_inner]
    far = [pb_outer, pb_inner, pc_outer, pc_inner]

    with jax.named_scope("planes"):
        came = []
        for step in range(5):
            if step == 0:
                load = jnp.where(first, away[0], near[0])
                sends = lambda second, early: not second or early
            elif step < 4:
                load = jnp.where(first, away[step], jnp.where(same, far[step - 1], near[step]))
                sends = lambda second, early: True
            else:
                load = far[3]
                sends = lambda second, early: second and not early
            came.append(between_planes(load, sends))

    with jax.named_scope("finish"):
        done_first = [halves(m + c) for m, c in zip(mine, came[:4])]
        done_second = [
            halves(jnp.where(same, n + c0, f + c1))
            for n, f, c0, c1 in zip(near, far, came[:4], came[1:])
        ]
        (f0p, f0q), (f1p, f1q), (f2p, f2q), (f3p, f3q) = done_first
        (s0p, s0q), (s1p, s1q), (s2p, s2q), (s3p, s3q) = done_second
        one = jnp.where(
            first, jnp.stack([f0p, f1p, f3p, f1q]), jnp.stack([s0p, s1p, s1q, s0q])
        ).astype(jnp.bfloat16)
        two = jnp.where(
            first, jnp.stack([f0q, f2p, f3q, f2q]), jnp.stack([s2p, s3p, s3q, s2q])
        ).astype(jnp.bfloat16)
        column = jnp.where(same, x, x ^ 3)
        keeps_one = (column % 2 == 0) == first
        stay = jnp.where(keeps_one, one, two)
        got = between_cores(jnp.where(keeps_one, two, one))
        rows = jnp.concatenate(
            [jnp.where(first, stay, got), jnp.where(first, got, stay)], 1
        )
        rows = jnp.where(y % 2 == 1, jnp.stack([rows[1], rows[0], rows[3], rows[2]]), rows)
        rows = jnp.where(y // 2 == 1, jnp.stack([rows[2], rows[3], rows[0], rows[1]]), rows)
        rows = rows.reshape(4 * ij_dev, rows.shape[2])
        index = red * rows.shape[0] + jnp.arange(rows.shape[0], dtype=jnp.int32)
        return jnp.where((index < live)[:, None], rows, jnp.zeros((), rows.dtype))


def solution(mesh):
    in_specs = (P("blk", "red"), P("blk", "red"), P())
    out_specs = P("red", "blk")
    return jax.shard_map(
        on_device, mesh=mesh, in_specs=in_specs, out_specs=out_specs, check_vma=False
    )
```

```python
import jax
import jax.numpy as jnp
from jax import lax
from jax.sharding import PartitionSpec as P

GROUP = 16
LANES = 128
STEPS = (60, 32, 16, 8, 4, 2, 1)


def exponents(largest, limit):
    scale = jnp.ones_like(largest)
    exponent = jnp.zeros_like(largest)
    for step in STEPS:
        fits = largest * scale * 2.0**step <= limit
        scale = jnp.where(fits, scale * 2.0**step, scale)
        exponent = jnp.where(fits, exponent + step, exponent)
    return scale, exponent


def unscale(exponent):
    left = exponent.astype(jnp.float32)
    factor = jnp.ones_like(left)
    for step in STEPS:
        taken = left >= step
        factor = jnp.where(taken, factor * 2.0**-step, factor)
        left = jnp.where(taken, left - step, left)
    return factor


def scaled_rows(block):
    wide = block.astype(jnp.float32)
    scale, exponent = exponents(jnp.max(jnp.abs(wide), axis=1, keepdims=True), 32768.0)
    tail = jnp.broadcast_to(exponent, (block.shape[0], LANES))
    return jnp.concatenate([(wide * scale).astype(jnp.float16), tail.astype(jnp.float16)], 1)


def across(block, distance):
    return lax.ppermute(
        block, "red", [(r, r ^ distance) for r in range(lax.axis_size("red"))]
    )


def on_device(amplitudes, integrals, occ_live):
    ij_dev, cd_dev = amplitudes.shape
    n_blk = lax.axis_size("blk")
    planes = [[s * GROUP + m for m in range(GROUP)] for s in range(n_blk // GROUP)]
    blk, red = lax.axis_index("blk"), lax.axis_index("red")
    z_half, core = red // 2, red % 2
    sector = blk // GROUP
    live = jnp.sum(jnp.where(jnp.arange(occ_live.shape[0]) == sector, occ_live, 0))

    gathered = lax.all_gather(
        scaled_rows(amplitudes), "blk", axis_index_groups=planes, axis=0, tiled=True
    )
    product = lax.dot_general(
        gathered[:, :cd_dev].astype(jnp.bfloat16),
        integrals,
        (((1,), (1,)), ((), ())),
        preferred_element_type=jnp.float32,
    )
    product = product * unscale(gathered[:, cd_dev : cd_dev + 1])
    owners = product.reshape(4, 4 * ij_dev, product.shape[1])

    def summed_over_cores(z):
        mine = lax.dynamic_index_in_dim(owners, 2 * z + core, 0, keepdims=False)
        other = lax.dynamic_index_in_dim(owners, 2 * z + 1 - core, 0, keepdims=False)
        return mine + across(other, 1)

    away = summed_over_cores(1 - z_half)
    scale, exponent = exponents(jnp.max(jnp.abs(away), axis=0, keepdims=True), 32767.0)
    tail = jnp.broadcast_to(exponent, (16, away.shape[1]))
    load = jnp.concatenate([jnp.round(away * scale), tail], 0).astype(jnp.int16)
    came = across(load, 2)
    came = came[: away.shape[0]].astype(jnp.float32) * unscale(came[away.shape[0] : away.shape[0] + 1])
    summed = summed_over_cores(z_half) + came
    index = red * summed.shape[0] + jnp.arange(summed.shape[0], dtype=jnp.int32)
    kept = jnp.where((index < live)[:, None], summed, jnp.zeros((), jnp.float32))
    return kept.astype(jnp.bfloat16)


def solution(mesh):
    in_specs = (P("blk", "red"), P("blk", "red"), P())
    out_specs = P("red", "blk")
    return jax.shard_map(
        on_device, mesh=mesh, in_specs=in_specs, out_specs=out_specs, check_vma=False
    )
```

```python
import jax
import jax.numpy as jnp
from jax import lax
from jax.sharding import PartitionSpec as P

GROUP = 16
LANES = 128
STEPS = (60, 32, 16, 8, 4, 2, 1)


def exponents(largest, limit):
    scale = jnp.ones_like(largest)
    exponent = jnp.zeros_like(largest)
    for step in STEPS:
        fits = largest * scale * 2.0**step <= limit
        scale = jnp.where(fits, scale * 2.0**step, scale)
        exponent = jnp.where(fits, exponent + step, exponent)
    return scale, exponent


def unscale(exponent):
    left = exponent.astype(jnp.float32)
    factor = jnp.ones_like(left)
    for step in STEPS:
        taken = left >= step
        factor = jnp.where(taken, factor * 2.0**-step, factor)
        left = jnp.where(taken, left - step, left)
    return factor


def scaled_rows(block):
    wide = block.astype(jnp.float32)
    scale, exponent = exponents(jnp.max(jnp.abs(wide), axis=1, keepdims=True), 32768.0)
    tail = jnp.broadcast_to(exponent, (block.shape[0], LANES))
    return jnp.concatenate([(wide * scale).astype(jnp.float16), tail.astype(jnp.float16)], 1)


def across(block, distance, pieces=1):
    route = [(r, r ^ distance) for r in range(lax.axis_size("red"))]
    moved = [lax.ppermute(piece, "red", route) for piece in jnp.split(block, pieces, 0)]
    return jnp.concatenate(moved, 0)


def on_device(amplitudes, integrals, occ_live):
    ij_dev, cd_dev = amplitudes.shape
    n_blk = lax.axis_size("blk")
    planes = [[s * GROUP + m for m in range(GROUP)] for s in range(n_blk // GROUP)]
    blk, red = lax.axis_index("blk"), lax.axis_index("red")
    z_half, core = red // 2, red % 2
    sector = blk // GROUP
    live = jnp.sum(jnp.where(jnp.arange(occ_live.shape[0]) == sector, occ_live, 0))

    gathered = lax.all_gather(
        scaled_rows(amplitudes), "blk", axis_index_groups=planes, axis=0, tiled=True
    )
    product = lax.dot_general(
        gathered[:, :cd_dev].astype(jnp.bfloat16),
        integrals,
        (((1,), (1,)), ((), ())),
        preferred_element_type=jnp.float32,
    )
    product = product * unscale(gathered[:, cd_dev : cd_dev + 1])
    owners = [product[4 * ij_dev * r : 4 * ij_dev * (r + 1)] for r in range(4)]

    def summed_over_cores(low, pieces):
        even, odd = (jnp.where(low, owners[r], owners[r + 2]) for r in (0, 1))
        return jnp.where(core == 0, even, odd) + across(jnp.where(core == 0, odd, even), 1, pieces)

    away = summed_over_cores(z_half == 1, 1)
    scale, exponent = exponents(jnp.max(jnp.abs(away), axis=0, keepdims=True), 32767.0)
    tail = jnp.broadcast_to(exponent, (16, away.shape[1]))
    load = jnp.concatenate([jnp.round(away * scale), tail], 0).astype(jnp.int16)
    came = across(load, 2)
    came = came[: away.shape[0]].astype(jnp.float32) * unscale(came[away.shape[0] : away.shape[0] + 1])
    summed = summed_over_cores(z_half == 0, 2) + came
    index = red * summed.shape[0] + jnp.arange(summed.shape[0], dtype=jnp.int32)
    kept = jnp.where((index < live)[:, None], summed, jnp.zeros((), jnp.float32))
    return kept.astype(jnp.bfloat16)


def solution(mesh):
    in_specs = (P("blk", "red"), P("blk", "red"), P())
    out_specs = P("red", "blk")
    return jax.shard_map(
        on_device, mesh=mesh, in_specs=in_specs, out_specs=out_specs, check_vma=False
    )
```

```python
import jax
import jax.numpy as jnp
from jax import lax
from jax.sharding import PartitionSpec as P

GROUP = 16
LANES = 128
RAISE = 12
STEPS = (60, 32, 16, 8, 4, 2, 1)


def exponents(largest, limit):
    scale = jnp.ones_like(largest)
    exponent = jnp.zeros_like(largest)
    for step in STEPS:
        fits = largest * scale * 2.0**step <= limit
        scale = jnp.where(fits, scale * 2.0**step, scale)
        exponent = jnp.where(fits, exponent + step, exponent)
    return scale, exponent


def unscale(exponent):
    left = exponent.astype(jnp.float32)
    factor = jnp.ones_like(left)
    for step in STEPS:
        taken = left >= step
        factor = jnp.where(taken, factor * 2.0**-step, factor)
        left = jnp.where(taken, left - step, left)
    return factor


def scaled_rows(block):
    near = lax.optimization_barrier(block * 2**RAISE)
    wide = near.astype(jnp.float32)
    scale, exponent = exponents(jnp.max(jnp.abs(wide), axis=1, keepdims=True), 32768.0)
    tail = jnp.broadcast_to(exponent, (block.shape[0], LANES))
    return jnp.concatenate([(wide * scale).astype(jnp.float16), tail.astype(jnp.float16)], 1)


def across(block, distance, pieces=1):
    route = [(r, r ^ distance) for r in range(lax.axis_size("red"))]
    moved = [lax.ppermute(piece, "red", route) for piece in jnp.split(block, pieces, 0)]
    return jnp.concatenate(moved, 0)


def on_device(amplitudes, integrals, occ_live):
    ij_dev, cd_dev = amplitudes.shape
    n_blk = lax.axis_size("blk")
    planes = [[s * GROUP + m for m in range(GROUP)] for s in range(n_blk // GROUP)]
    blk, red = lax.axis_index("blk"), lax.axis_index("red")
    z_half, core = red // 2, red % 2
    sector = blk // GROUP
    live = jnp.sum(jnp.where(jnp.arange(occ_live.shape[0]) == sector, occ_live, 0))

    gathered = lax.all_gather(
        scaled_rows(amplitudes), "blk", axis_index_groups=planes, axis=0, tiled=True
    )
    product = lax.dot_general(
        gathered[:, :cd_dev].astype(jnp.bfloat16),
        integrals,
        (((1,), (1,)), ((), ())),
        preferred_element_type=jnp.float32,
    )
    product = product * 2.0**-RAISE * unscale(gathered[:, cd_dev : cd_dev + 1])
    owners = [product[4 * ij_dev * r : 4 * ij_dev * (r + 1)] for r in range(4)]

    def summed_over_cores(low, pieces):
        even, odd = (jnp.where(low, owners[r], owners[r + 2]) for r in (0, 1))
        return jnp.where(core == 0, even, odd) + across(jnp.where(core == 0, odd, even), 1, pieces)

    away = summed_over_cores(z_half == 1, 1)
    scale, exponent = exponents(jnp.max(jnp.abs(away), axis=0, keepdims=True), 32767.0)
    tail = jnp.broadcast_to(exponent, (8, away.shape[1]))
    load = jnp.concatenate([jnp.round(away * scale), tail], 0).astype(jnp.int16)
    came = across(load, 2)
    came = came[: away.shape[0]].astype(jnp.float32) * unscale(came[away.shape[0] : away.shape[0] + 1])
    summed = summed_over_cores(z_half == 0, 2) + came
    index = red * summed.shape[0] + jnp.arange(summed.shape[0], dtype=jnp.int32)
    kept = jnp.where((index < live)[:, None], summed, jnp.zeros((), jnp.float32))
    return kept.astype(jnp.bfloat16)


def solution(mesh):
    in_specs = (P("blk", "red"), P("blk", "red"), P())
    out_specs = P("red", "blk")
    return jax.shard_map(
        on_device, mesh=mesh, in_specs=in_specs, out_specs=out_specs, check_vma=False
    )
```

```python
import jax
import jax.numpy as jnp
from jax import lax
from jax.sharding import PartitionSpec as P

GROUP = 16
LANES = 128
RAISE = 12
STEPS = (60, 32, 16, 8, 4, 2, 1)


def exponents(largest, limit):
    scale = jnp.ones_like(largest)
    exponent = jnp.zeros_like(largest)
    for step in STEPS:
        fits = largest * scale * 2.0**step <= limit
        scale = jnp.where(fits, scale * 2.0**step, scale)
        exponent = jnp.where(fits, exponent + step, exponent)
    return scale, exponent


def unscale(exponent):
    left = exponent.astype(jnp.float32)
    factor = jnp.ones_like(left)
    for step in STEPS:
        taken = left >= step
        factor = jnp.where(taken, factor * 2.0**-step, factor)
        left = jnp.where(taken, left - step, left)
    return factor


def scaled_rows(block):
    near = lax.optimization_barrier(block * 2**RAISE)
    wide = near.astype(jnp.float32)
    scale, exponent = exponents(jnp.max(jnp.abs(wide), axis=1, keepdims=True), 32768.0)
    tail = jnp.broadcast_to(exponent, (block.shape[0], LANES))
    return jnp.concatenate([(wide * scale).astype(jnp.float16), tail.astype(jnp.float16)], 1)


def across(block, distance, pieces=1):
    route = [(r, r ^ distance) for r in range(lax.axis_size("red"))]
    moved = [lax.ppermute(piece, "red", route) for piece in jnp.split(block, pieces, 0)]
    return jnp.concatenate(moved, 0)


def on_device(amplitudes, integrals, occ_live):
    ij_dev, cd_dev = amplitudes.shape
    n_blk = lax.axis_size("blk")
    planes = [[s * GROUP + m for m in range(GROUP)] for s in range(n_blk // GROUP)]
    blk, red = lax.axis_index("blk"), lax.axis_index("red")
    z_half, core = red // 2, red % 2
    sector = blk // GROUP
    live = jnp.sum(jnp.where(jnp.arange(occ_live.shape[0]) == sector, occ_live, 0))

    gathered = lax.all_gather(
        scaled_rows(amplitudes), "blk", axis_index_groups=planes, axis=0, tiled=True
    )
    product = lax.dot_general(
        gathered[:, :cd_dev].astype(jnp.bfloat16),
        integrals,
        (((1,), (1,)), ((), ())),
        preferred_element_type=jnp.float32,
    )
    product = product * 2.0**-RAISE * unscale(gathered[:, cd_dev : cd_dev + 1])
    owners = [product[4 * ij_dev * r : 4 * ij_dev * (r + 1)] for r in range(4)]

    def summed_over_cores(low, pieces):
        even, odd = (jnp.where(low, owners[r], owners[r + 2]) for r in (0, 1))
        return jnp.where(core == 0, even, odd) + across(jnp.where(core == 0, odd, even), 1, pieces)

    def live_rows(block, owner):
        index = owner * block.shape[0] + jnp.arange(block.shape[0], dtype=jnp.int32)
        return jnp.where((index < live)[:, None], block, jnp.zeros((), block.dtype))

    away = live_rows(summed_over_cores(z_half == 1, 1), red ^ 2)
    scale, exponent = exponents(jnp.max(jnp.abs(away), axis=0, keepdims=True), 32767.0)
    tail = jnp.broadcast_to(exponent, (8, away.shape[1]))
    load = jnp.concatenate([jnp.round(away * scale), tail], 0).astype(jnp.int16)
    came = across(load, 2)
    came = came[: away.shape[0]].astype(jnp.float32) * unscale(came[away.shape[0] : away.shape[0] + 1])
    summed = summed_over_cores(z_half == 0, 2) + came
    return live_rows(summed, red).astype(jnp.bfloat16)


def solution(mesh):
    in_specs = (P("blk", "red"), P("blk", "red"), P())
    out_specs = P("red", "blk")
    return jax.shard_map(
        on_device, mesh=mesh, in_specs=in_specs, out_specs=out_specs, check_vma=False
    )
```

```python
import jax
import jax.numpy as jnp
from jax import lax
from jax.sharding import PartitionSpec as P

GROUP = 16
LANES = 128
RAISE = 12
STEPS = (60, 32, 16, 8, 4, 2, 1)
ROW_STEPS = (64, 32, 16, 8, 4)


def exponents(largest, limit, steps=STEPS):
    scale = jnp.ones_like(largest)
    exponent = jnp.zeros_like(largest)
    for step in steps:
        fits = largest * scale * 2.0**step <= limit
        scale = jnp.where(fits, scale * 2.0**step, scale)
        exponent = jnp.where(fits, exponent + step, exponent)
    return scale, exponent


def unscale(exponent):
    left = exponent.astype(jnp.float32)
    factor = jnp.ones_like(left)
    for step in STEPS:
        taken = left >= step
        factor = jnp.where(taken, factor * 2.0**-step, factor)
        left = jnp.where(taken, left - step, left)
    return factor


def scaled_rows(block):
    near = lax.optimization_barrier(block * 2**RAISE)
    wide = near.astype(jnp.float32)
    scale, exponent = exponents(jnp.max(jnp.abs(wide), axis=1, keepdims=True), 32768.0, ROW_STEPS)
    lane = jnp.arange(LANES, dtype=jnp.float32)[None, :]
    left = exponent - 8.0 * lane
    tail = jnp.where(left >= 8.0, 2.0**-8, jnp.where(left >= 4.0, 2.0**-4, 1.0))
    return jnp.concatenate([(wide * scale).astype(jnp.float16), tail.astype(jnp.float16)], 1)


def across(block, distance, pieces=1):
    route = [(r, r ^ distance) for r in range(lax.axis_size("red"))]
    moved = [lax.ppermute(piece, "red", route) for piece in jnp.split(block, pieces, 0)]
    return jnp.concatenate(moved, 0)


def on_device(amplitudes, integrals, occ_live):
    ij_dev, cd_dev = amplitudes.shape
    n_blk = lax.axis_size("blk")
    planes = [[s * GROUP + m for m in range(GROUP)] for s in range(n_blk // GROUP)]
    blk, red = lax.axis_index("blk"), lax.axis_index("red")
    z_half, core = red // 2, red % 2
    sector = blk // GROUP
    live = jnp.sum(jnp.where(jnp.arange(occ_live.shape[0]) == sector, occ_live, 0))

    gathered = lax.all_gather(
        scaled_rows(amplitudes), "blk", axis_index_groups=planes, axis=0, tiled=True
    )
    product = lax.dot_general(
        gathered[:, :cd_dev].astype(jnp.bfloat16),
        integrals,
        (((1,), (1,)), ((), ())),
        preferred_element_type=jnp.float32,
    )
    product = product * 2.0**-RAISE * jnp.prod(gathered[:, cd_dev:].astype(jnp.float32), axis=1, keepdims=True)
    owners = [product[4 * ij_dev * r : 4 * ij_dev * (r + 1)] for r in range(4)]

    def summed_over_cores(low, pieces):
        even, odd = (jnp.where(low, owners[r], owners[r + 2]) for r in (0, 1))
        return jnp.where(core == 0, even, odd) + across(jnp.where(core == 0, odd, even), 1, pieces)

    def live_rows(block, owner):
        index = owner * block.shape[0] + jnp.arange(block.shape[0], dtype=jnp.int32)
        return jnp.where((index < live)[:, None], block, jnp.zeros((), block.dtype))

    away = live_rows(summed_over_cores(z_half == 1, 1), red ^ 2)
    scale, exponent = exponents(jnp.max(jnp.abs(away), axis=0, keepdims=True), 32767.0)
    tail = jnp.broadcast_to(exponent, (8, away.shape[1]))
    load = jnp.concatenate([jnp.round(away * scale), tail], 0).astype(jnp.int16)
    came = across(load, 2)
    came = came[: away.shape[0]].astype(jnp.float32) * unscale(came[away.shape[0] : away.shape[0] + 1])
    summed = summed_over_cores(z_half == 0, 2) + came
    return live_rows(summed, red).astype(jnp.bfloat16)


def solution(mesh):
    in_specs = (P("blk", "red"), P("blk", "red"), P())
    out_specs = P("red", "blk")
    return jax.shard_map(
        on_device, mesh=mesh, in_specs=in_specs, out_specs=out_specs, check_vma=False
    )
```

```python
import jax
import jax.numpy as jnp
from jax import lax
from jax.sharding import PartitionSpec as P

GROUP = 16
LANES = 128
RAISE = 12
STEPS = (60, 32, 16, 8, 4, 2, 1)
ROW_STEPS = (64, 32, 16, 8, 4)


def exponents(largest, limit, steps=STEPS):
    scale = jnp.ones_like(largest)
    exponent = jnp.zeros_like(largest)
    for step in steps:
        fits = largest * scale * 2.0**step <= limit
        scale = jnp.where(fits, scale * 2.0**step, scale)
        exponent = jnp.where(fits, exponent + step, exponent)
    return scale, exponent


def unscale(exponent):
    return jnp.exp2(-exponent.astype(jnp.float32))


def scaled_rows(block):
    near = lax.optimization_barrier(block * 2**RAISE)
    wide = near.astype(jnp.float32)
    scale, exponent = exponents(jnp.max(jnp.abs(wide), axis=1, keepdims=True), 32768.0, ROW_STEPS)
    lane = jnp.arange(LANES, dtype=jnp.float32)[None, :]
    left = exponent - 8.0 * lane
    tail = jnp.where(left >= 8.0, 2.0**-8, jnp.where(left >= 4.0, 2.0**-4, 1.0))
    return jnp.concatenate([(wide * scale).astype(jnp.float16), tail.astype(jnp.float16)], 1)


def across(block, distance, pieces=1):
    route = [(r, r ^ distance) for r in range(lax.axis_size("red"))]
    moved = [lax.ppermute(piece, "red", route) for piece in jnp.split(block, pieces, 0)]
    return jnp.concatenate(moved, 0)


def on_device(amplitudes, integrals, occ_live):
    ij_dev, cd_dev = amplitudes.shape
    n_blk = lax.axis_size("blk")
    planes = [[s * GROUP + m for m in range(GROUP)] for s in range(n_blk // GROUP)]
    blk, red = lax.axis_index("blk"), lax.axis_index("red")
    z_half, core = red // 2, red % 2
    sector = blk // GROUP
    live = jnp.sum(jnp.where(jnp.arange(occ_live.shape[0]) == sector, occ_live, 0))

    gathered = lax.all_gather(
        scaled_rows(amplitudes), "blk", axis_index_groups=planes, axis=0, tiled=True
    )
    product = lax.dot_general(
        gathered[:, :cd_dev].astype(jnp.bfloat16),
        integrals,
        (((1,), (1,)), ((), ())),
        preferred_element_type=jnp.float32,
    )
    product = product * 2.0**-RAISE * jnp.prod(gathered[:, cd_dev:].astype(jnp.float32), axis=1, keepdims=True)
    owners = [product[4 * ij_dev * r : 4 * ij_dev * (r + 1)] for r in range(4)]

    def summed_over_cores(low, pieces):
        even, odd = (jnp.where(low, owners[r], owners[r + 2]) for r in (0, 1))
        return jnp.where(core == 0, even, odd) + across(jnp.where(core == 0, odd, even), 1, pieces)

    def live_rows(block, owner):
        index = owner * block.shape[0] + jnp.arange(block.shape[0], dtype=jnp.int32)
        return jnp.where((index < live)[:, None], block, jnp.zeros((), block.dtype))

    away = live_rows(summed_over_cores(z_half == 1, 1), red ^ 2)
    scale, exponent = exponents(jnp.max(jnp.abs(away), axis=0, keepdims=True), 32767.0)
    tail = jnp.broadcast_to(exponent, (8, away.shape[1]))
    load = jnp.concatenate([jnp.round(away * scale), tail], 0).astype(jnp.int16)
    came = across(load, 2)
    came = came[: away.shape[0]].astype(jnp.float32) * unscale(came[away.shape[0] : away.shape[0] + 1])
    summed = summed_over_cores(z_half == 0, 2) + came
    return live_rows(summed, red).astype(jnp.bfloat16)


def solution(mesh):
    in_specs = (P("blk", "red"), P("blk", "red"), P())
    out_specs = P("red", "blk")
    return jax.shard_map(
        on_device, mesh=mesh, in_specs=in_specs, out_specs=out_specs, check_vma=False
    )
```

```python
import jax
import jax.numpy as jnp
from jax import lax
from jax.sharding import PartitionSpec as P

GROUP = 16
LANES = 128
RAISE = 12
STEPS = (60, 32, 16, 8, 4, 2, 1)
ROW_STEPS = (48, 32, 16, 8, 4)


def exponents(largest, limit, steps=STEPS):
    scale = jnp.ones_like(largest)
    exponent = jnp.zeros_like(largest)
    for step in steps:
        fits = largest * scale * 2.0**step <= limit
        scale = jnp.where(fits, scale * 2.0**step, scale)
        exponent = jnp.where(fits, exponent + step, exponent)
    return scale, exponent


def unscale(exponent):
    left = exponent.astype(jnp.float32)
    factor = jnp.ones_like(left)
    for step in STEPS:
        taken = left >= step
        factor = jnp.where(taken, factor * 2.0**-step, factor)
        left = jnp.where(taken, left - step, left)
    return factor


def scaled_rows(block):
    near = lax.optimization_barrier(block * 2**RAISE)
    wide = near.astype(jnp.float32)
    scale, exponent = exponents(jnp.max(jnp.abs(wide), axis=1, keepdims=True), 32768.0, ROW_STEPS)
    lane = jnp.arange(LANES, dtype=jnp.float32)[None, :]
    left = exponent + RAISE - 8.0 * lane
    tail = jnp.where(left >= 8.0, 2.0**-8, jnp.where(left >= 4.0, 2.0**-4, 1.0))
    return jnp.concatenate([(wide * scale).astype(jnp.float16), tail.astype(jnp.float16)], 1)


def across(block, distance, pieces=1):
    route = [(r, r ^ distance) for r in range(lax.axis_size("red"))]
    moved = [lax.ppermute(piece, "red", route) for piece in jnp.split(block, pieces, 0)]
    return jnp.concatenate(moved, 0)


def on_device(amplitudes, integrals, occ_live):
    ij_dev, cd_dev = amplitudes.shape
    n_blk = lax.axis_size("blk")
    planes = [[s * GROUP + m for m in range(GROUP)] for s in range(n_blk // GROUP)]
    blk, red = lax.axis_index("blk"), lax.axis_index("red")
    z_half, core = red // 2, red % 2
    sector = blk // GROUP
    live = jnp.sum(jnp.where(jnp.arange(occ_live.shape[0]) == sector, occ_live, 0))

    gathered = lax.all_gather(
        scaled_rows(amplitudes), "blk", axis_index_groups=planes, axis=0, tiled=True
    )
    product = lax.dot_general(
        gathered[:, :cd_dev].astype(jnp.bfloat16),
        integrals,
        (((1,), (1,)), ((), ())),
        preferred_element_type=jnp.float32,
    )
    product = product * jnp.prod(gathered[:, cd_dev:].astype(jnp.float32), axis=1, keepdims=True)
    owners = [product[4 * ij_dev * r : 4 * ij_dev * (r + 1)] for r in range(4)]

    def summed_over_cores(low, pieces):
        even, odd = (jnp.where(low, owners[r], owners[r + 2]) for r in (0, 1))
        return jnp.where(core == 0, even, odd) + across(jnp.where(core == 0, odd, even), 1, pieces)

    def live_rows(block, owner):
        index = owner * block.shape[0] + jnp.arange(block.shape[0], dtype=jnp.int32)
        return jnp.where((index < live)[:, None], block, jnp.zeros((), block.dtype))

    away = live_rows(summed_over_cores(z_half == 1, 1), red ^ 2)
    scale, exponent = exponents(jnp.max(jnp.abs(away), axis=0, keepdims=True), 32767.0)
    tail = jnp.broadcast_to(exponent, (8, away.shape[1]))
    load = jnp.concatenate([jnp.round(away * scale), tail], 0).astype(jnp.int16)
    came = across(load, 2)
    came = came[: away.shape[0]].astype(jnp.float32) * unscale(came[away.shape[0] : away.shape[0] + 1])
    summed = summed_over_cores(z_half == 0, 2) + came
    return live_rows(summed, red).astype(jnp.bfloat16)


def solution(mesh):
    in_specs = (P("blk", "red"), P("blk", "red"), P())
    out_specs = P("red", "blk")
    return jax.shard_map(
        on_device, mesh=mesh, in_specs=in_specs, out_specs=out_specs, check_vma=False
    )
```
